32 devices in a mesh: dm: 16 (over z, x, core), beam: 2 (over y).
Axes of the slice: x: 2, y: 2, z: 4, core: 2. Of those that a mesh axis runs over, the one named last changes fastest.
Arguments:
- voltages: bfloat16 [4096, 2, 2, 256], P(('beam', 'dm')), may hold values from -6 to 6
- responses: bfloat16 [64, 4096, 2, 256], P('dm', 'beam'), may hold values from -6 to 6
- chirp_len: int32 [64], P('dm'), may hold values from 1 to 128, as said below
Outputs:
- detected: bfloat16 [64, 2, 262144], P('dm', 'beam')
The draws below stay inside these ranges and needn't reach their ends.
Inputs may be any that keep to these rules, and one draw needn't show every extreme that they name: `chirp_len`: some trial has the longest chirp 256 // 2 and some trial a chirp of 1 sample.
All inputs are finite; a program needn't handle non-finite values.
Results may differ from the reference program's by a relative error of at most 0.0054.
Values may be sent and summed in bfloat16 or wider, within the bound.
A program may use at most 128 MiB of HBM per device.

```python
import math
import jax
import jax.numpy as jnp
from jax import lax

CH = 4096
L = 256
RATE = 4
DMS = 64
BEAMS = 2
TOUT = 64


def draw_chirp_len(key, part):
    values = jax.random.randint(key, (DMS,), 1, L // 2 + 1, dtype=jnp.int32)
    chosen = jax.random.randint(jax.random.fold_in(key, 7), (), 0, DMS, dtype=jnp.int32)
    values = values.at[chosen].set(L // 2)
    values = values.at[(chosen + 1) % DMS].set(1)
    return values


def block_levels(own_key, shape, pieces, smallest, top_value):
    def one(dim, parts):
        heights = jax.random.uniform(jax.random.fold_in(jax.random.fold_in(own_key, 6), dim), (parts,), jnp.float32, smallest / len(pieces), top_value / len(pieces))
        return jnp.repeat(jnp.exp(heights), shape[dim] // parts).reshape((-1,) + (1,) * (len(shape) - dim - 1))

    loudness = one(*pieces[0])
    for cut in pieces[1:]:
        loudness = loudness * one(*cut)
    return loudness


def bell_draw(rng, shape, width, limit, pieces=(), held_as=jnp.bfloat16):
    array = width * jax.random.normal(rng, shape, jnp.float32)
    if pieces:
        array = array * block_levels(rng, shape, pieces, -0.22, 0.18)
    return jnp.clip(array, -limit, limit).astype(held_as)


def setup_inputs(seed: int = 0) -> dict:
    arg_keys = jax.random.split(jax.random.key(seed), 4)
    return {
        "voltages": bell_draw(arg_keys[0], (CH, BEAMS, 2, L), 0.7, 6.0, ((0, 32),)),
        "responses": bell_draw(arg_keys[1], (DMS, CH, 2, L), 0.7, 6.0, ((0, 16), (1, 2))),
        "chirp_len": draw_chirp_len(jax.random.fold_in(arg_keys[3], 71), 0),
    }


def dft_tables(length):
    sample = jnp.arange(length, dtype=jnp.int32)
    phases = sample[:, None] * sample[None, :] % length
    angles = phases.astype(jnp.float32) * (2.0 * math.pi / length)
    cosine = jnp.cos(angles) / math.sqrt(length)
    sine_part = jnp.sin(angles) / math.sqrt(length)
    forward = jnp.concatenate([jnp.concatenate([cosine, -sine_part], 1), jnp.concatenate([sine_part, cosine], 1)], 0)
    backward = jnp.concatenate([jnp.concatenate([cosine, sine_part], 1), jnp.concatenate([-sine_part, cosine], 1)], 0)
    return (forward.astype(jnp.bfloat16), backward.astype(jnp.bfloat16))

def spectrum(signal, forward):
    length = signal.shape[-1]
    flattened = signal.reshape(-1, 2 * length)
    result = jnp.dot(flattened, forward, preferred_element_type=jnp.float32)
    return result.astype(jnp.bfloat16).reshape(signal.shape)

def detect(spectra, response, lengths, backward, rate):
    chans = spectra.shape[0]
    beam_count = spectra.shape[1]
    length = spectra.shape[-1]
    samples_out = length // rate
    spec_re = spectra[:, :, 0, :].astype(jnp.float32)
    spec_im = spectra[:, :, 1, :].astype(jnp.float32)
    sample = jnp.arange(length, dtype=jnp.int32)

    def one_trial(trial):
        filter_row, chirp = trial
        resp_re = filter_row[:, 0, :].astype(jnp.float32)[:, None, :]
        resp_im = filter_row[:, 1, :].astype(jnp.float32)[:, None, :]
        real_part = resp_re * spec_re - resp_im * spec_im
        imag_part = resp_re * spec_im + resp_im * spec_re
        joined = jnp.concatenate([real_part, imag_part], -1).astype(jnp.bfloat16)
        series = jnp.dot(joined.reshape(-1, 2 * length), backward, preferred_element_type=jnp.float32)
        series = series.reshape(chans, beam_count, 2 * length)
        powers = series[..., :length] ** 2 + series[..., length:] ** 2
        valid_mask = sample >= chirp
        powers = jnp.where(valid_mask[None, None, :], powers, jnp.float32(0.0))
        binned = powers.reshape(chans, beam_count, samples_out, rate).sum(-1) / rate
        return jnp.transpose(binned, (1, 0, 2)).astype(jnp.bfloat16)
    return lax.map(one_trial, (response, lengths))

def reference(voltages, responses, chirp_len):
    forward, backward = dft_tables(L)
    spectra = spectrum(voltages, forward)
    result = detect(spectra, responses, chirp_len, backward, RATE)
    return result.reshape(DMS, BEAMS, CH * TOUT)
```

```python
import functools
import math

import jax
import jax.numpy as jnp
import ml_dtypes
import numpy as np
from jax import lax
from jax.experimental import pallas as pl
from jax.experimental.pallas import tpu as pltpu
from jax.sharding import PartitionSpec as P

RATE = 4
LANES = 128
MESH = pl.DeviceIdType.MESH


def dft_tables(length):
    sample = np.arange(length)
    angles = (sample[:, None] * sample[None, :] % length) * (2.0 * math.pi / length)
    cosine = np.cos(angles) / math.sqrt(length)
    sine = np.sin(angles) / math.sqrt(length)
    forward = np.block([[cosine, -sine], [sine, cosine]])
    order = sample.reshape(-1, RATE).T.reshape(-1)
    cosine, sine = cosine[:, order], sine[:, order]
    backward = np.block([[cosine, sine], [-sine, cosine]])
    return [table.astype(np.float32).astype(ml_dtypes.bfloat16) for table in (forward, backward)]


def kernel(
    dm, beams, trials, chans, length,
    volt_ref, resp_ref, chirp_ref, fwd_ref, bwd_ref, out_ref,
    spec, resp, stage, rows_in, filt, rows_out,
    block_sem, far_sem, near_sem, core_sem, resp_sem, beam_send, beam_recv, own_sem,
):
    tiles = length // LANES
    half = chans // 2
    depth = dm // 4
    span = half * trials
    held = chans * tiles * 2
    me = lax.axis_index("dm")
    beam = lax.axis_index("beam")
    z, x, k = me // 4, (me // 2) % 2, me % 2

    def place(zz, xx, kk):
        return (zz * 2 + xx) * 2 + kk

    def plane(step):
        return (z + step) % depth

    def resp_copy(block):
        rows = pl.ds(block * held, held)
        return pltpu.make_async_copy(
            resp_ref.at[:, rows, :], resp.at[:, rows, :], resp_sem.at[block]
        )

    def send(block, sem, target):
        return pltpu.make_async_remote_copy(
            src_ref=spec.at[block],
            dst_ref=spec.at[block],
            send_sem=sem,
            recv_sem=block_sem.at[block],
            device_id={"dm": target},
            device_id_type=MESH,
        )

    def far(step):
        return send(me, far_sem.at[step - 1], place(plane(step), x, k))

    def near(step):
        return send(place(plane(step), x, k), near_sem.at[step], place(z, 1 - x, k))

    def across(step, side):
        column = (x + side) % 2
        block = place(plane(step), column, k)
        return send(block, core_sem.at[step * 2 + side], place(z, x, 1 - k))

    def arrived(block):
        pltpu.make_async_copy(spec.at[block], spec.at[block], block_sem.at[block]).wait()

    def beam_copy(offset, start, count):
        other = (beam + offset) % beams
        first = beam * (dm * span) + start
        return pltpu.make_async_remote_copy(
            src_ref=stage.at[other, pl.ds(start, count), :],
            dst_ref=out_ref.at[pl.ds(first, count), :],
            send_sem=beam_send.at[offset - 1],
            recv_sem=beam_recv.at[offset - 1],
            device_id={"beam": other},
            device_id_type=MESH,
        )

    def fetch(step, carry):
        plane_at = plane(step // 4)
        resp_copy(place(plane_at, (x + step % 4 // 2) % 2, (k + step % 2) % 2)).start()
        return carry

    lax.fori_loop(0, dm, fetch, 0)

    barrier = pltpu.get_barrier_semaphore()
    for step in range(1, depth):
        pl.semaphore_signal(
            barrier, inc=1, device_id={"dm": place(plane(step), x, k)}, device_id_type=MESH
        )
    pl.semaphore_signal(barrier, inc=1, device_id={"dm": place(z, 1 - x, k)}, device_id_type=MESH)
    pl.semaphore_signal(barrier, inc=1, device_id={"dm": place(z, x, 1 - k)}, device_id_type=MESH)
    for offset in range(1, beams):
        pl.semaphore_signal(
            barrier, inc=1, device_id={"beam": (beam + offset) % beams}, device_id_type=MESH
        )

    rows_in[...] = volt_ref[...].astype(jnp.float32)
    stride = 2 * beams * tiles * 2
    pieces = []
    for b in range(beams):
        for parity in range(2):
            first = (parity * beams + b) * tiles * 2
            pieces.append(jnp.concatenate(
                [rows_in[pl.ds(first + t * 2 + part, half, stride=stride), :]
                 for part in range(2) for t in range(tiles)], 1))
    signal = jnp.concatenate(pieces, 0).astype(jnp.bfloat16)
    spec[me] = jnp.dot(
        signal, fwd_ref[...], preferred_element_type=jnp.float32
    ).astype(jnp.bfloat16)

    pl.semaphore_wait(barrier, depth + beams)

    near(0).start()
    for step in range(1, depth):
        far(step).start()
    across(0, 0).start()

    column = lax.broadcasted_iota(jnp.int32, (1, length), 1)
    bins = length // RATE
    sample = column % bins * RATE + column // bins
    low = lax.broadcasted_iota(jnp.int32, (half, LANES), 1) < bins

    def detect(block):
        for d in range(trials):
            filt[d] = resp[d, pl.ds(block * held, held), :].astype(jnp.float32)
        for d in range(trials):
            taps = [[jnp.concatenate(
                [filt[d, pl.ds((parity * tiles + t) * 2 + part, half, stride=4 * tiles), :]
                 for t in range(tiles)], 1) for part in range(2)] for parity in range(2)]
            values = spec[block].astype(jnp.float32)
            pieces = []
            for b in range(beams):
                for parity in range(2):
                    at = (b * 2 + parity) * half
                    xr = values[at:at + half, :length]
                    xi = values[at:at + half, length:]
                    hr, hi = taps[parity]
                    pieces.append(
                        jnp.concatenate([hr * xr - hi * xi, hr * xi + hi * xr], 1)
                    )
            joined = jnp.concatenate(pieces, 0).astype(jnp.bfloat16)
            series = jnp.dot(joined, bwd_ref[...], preferred_element_type=jnp.float32)
            power = series[:, :length] * series[:, :length] + series[:, length:] * series[:, length:]
            power = jnp.where(sample >= chirp_ref[d], power, 0.0)
            total = power[:, :LANES]
            for t in range(1, tiles):
                total = total + power[:, t * LANES:(t + 1) * LANES]
            for b in range(beams):
                at = b * 2 * half
                even = total[at:at + half]
                odd = total[at + half:at + 2 * half]
                straight = jnp.where(low, even, odd)
                turned = pltpu.roll(jnp.where(low, odd, even), bins, 1)
                rows_out[b, pl.ds(d, half, stride=trials), :] = (straight + turned) * (1.0 / RATE)
        for b in range(beams):
            stage[b, pl.ds(block * span, span), :] = rows_out[b].astype(jnp.bfloat16)

    def body(step, carry):
        group, turn = step // 4, step % 4
        block = place(plane(group), (x + turn // 2) % 2, (k + turn % 2) % 2)

        @pl.when(turn > 0)
        def _():
            arrived(block)

        @pl.when(turn == 2)
        def _():
            across(group, 1).start()

        @pl.when((turn == 1) & (group < depth - 1))
        def _():
            arrived(place(plane(group + 1), x, k))
            near(group + 1).start()
            across(group + 1, 0).start()

        resp_copy(block).wait()
        detect(block)
        for offset in range(1, beams):
            beam_copy(offset, block * span, span).start()
        return carry

    lax.fori_loop(0, dm, body, 0)

    own = pltpu.make_async_copy(
        stage.at[beam], out_ref.at[pl.ds(beam * (dm * span), dm * span), :], own_sem
    )
    own.start()

    for step in range(1, depth):
        far(step).wait_send()
    for step in range(depth):
        near(step).wait_send()
        across(step, 0).wait_send()
        across(step, 1).wait_send()
    own.wait()
    for offset in range(1, beams):
        whole = beam_copy(offset, 0, dm * span)
        whole.wait_send()
        whole.wait_recv()


def shards(dm, beams, voltages, responses, chirp_len):
    chans, _, _, length = voltages.shape
    trials, group = responses.shape[:2]
    tiles = length // LANES
    forward, backward = dft_tables(length)

    def tiled(array):
        head = array.shape[:-2]
        array = array.reshape(head + (2, tiles, LANES))
        return jnp.swapaxes(array, -2, -3)

    volt = tiled(voltages).reshape(chans * beams * tiles * 2, LANES)
    resp = tiled(responses).reshape(trials, group * tiles * 2, LANES)
    span = chans // 2 * trials
    rows = beams * dm * span
    vmem = pl.BlockSpec(memory_space=pltpu.VMEM)
    anywhere = pl.BlockSpec(memory_space=pl.ANY)
    flops = 2 * (trials * group + chans) * beams * (2 * length) ** 2
    out = pl.pallas_call(
        functools.partial(kernel, dm, beams, trials, chans, length),
        out_shape=jax.ShapeDtypeStruct((rows, LANES), jnp.bfloat16),
        in_specs=[vmem, anywhere, pl.BlockSpec(memory_space=pltpu.SMEM), vmem, vmem],
        out_specs=anywhere,
        scratch_shapes=[
            pltpu.VMEM((dm, beams * chans, 2 * length), jnp.bfloat16),
            pltpu.VMEM(resp.shape, jnp.bfloat16),
            pltpu.VMEM((beams, dm * span, LANES), jnp.bfloat16),
            pltpu.VMEM(volt.shape, jnp.float32),
            pltpu.VMEM((trials, chans * tiles * 2, LANES), jnp.float32),
            pltpu.VMEM((beams, span, LANES), jnp.float32),
            pltpu.SemaphoreType.DMA((dm,)),
            pltpu.SemaphoreType.DMA((dm // 4,)),
            pltpu.SemaphoreType.DMA((dm // 4,)),
            pltpu.SemaphoreType.DMA((dm // 2,)),
            pltpu.SemaphoreType.DMA((dm,)),
            pltpu.SemaphoreType.DMA((beams,)),
            pltpu.SemaphoreType.DMA((beams,)),
            pltpu.SemaphoreType.DMA,
        ],
        compiler_params=pltpu.CompilerParams(
            collective_id=0, has_side_effects=True, vmem_limit_bytes=48 * 2**20
        ),
        cost_estimate=pl.CostEstimate(
            flops=flops, bytes_accessed=resp.size * 2 + rows * LANES * 2, transcendentals=0
        ),
    )(volt, resp, chirp_len, jnp.asarray(forward), jnp.asarray(backward))
    out = out.reshape(-1, trials, LANES)
    return jnp.swapaxes(out, 0, 1).reshape(trials, 1, -1)


def solution(mesh):
    placed = (P(("beam", "dm"), None, None, None), P("dm", "beam", None, None), P("dm"))
    return jax.shard_map(
        functools.partial(shards, mesh.shape["dm"], mesh.shape["beam"]),
        mesh=mesh, in_specs=placed, out_specs=P("dm", "beam", None), check_vma=False,
    )
```

```python
import functools
import math

import jax
import jax.numpy as jnp
import ml_dtypes
import numpy as np
from jax import lax
from jax.experimental import pallas as pl
from jax.experimental.pallas import tpu as pltpu
from jax.sharding import PartitionSpec as P

RATE = 4
LANES = 128
MESH = pl.DeviceIdType.MESH


def dft_tables(length):
    sample = np.arange(length)
    angles = (sample[:, None] * sample[None, :] % length) * (2.0 * math.pi / length)
    cosine = np.cos(angles) / math.sqrt(length)
    sine = np.sin(angles) / math.sqrt(length)
    forward = np.block([[cosine, -sine], [sine, cosine]])
    order = sample.reshape(-1, RATE).T.reshape(-1)
    cosine, sine = cosine[:, order], sine[:, order]
    backward = np.block([[cosine, sine], [-sine, cosine]])
    return [table.astype(np.float32).astype(ml_dtypes.bfloat16) for table in (forward, backward)]


def kernel(
    dm, beams, trials, chans, length,
    volt_hbm, resp_ref, chirp_hbm, fwd_hbm, bwd_hbm, out_ref,
    volt_ref, chirp_ref, fwd_ref, bwd_ref, spec, resp, stage, rows_in, filt, rows_out,
    block_sem, up_sem, down_sem, near_sem, core_sem, resp_sem, beam_send, beam_recv, own_sem, in_sem,
):
    tiles = length // LANES
    half = chans // 2
    depth = dm // 4
    span = half * trials
    held = chans * tiles * 2
    me = lax.axis_index("dm")
    beam = lax.axis_index("beam")
    z, x, k = me // 4, (me // 2) % 2, me % 2

    def place(zz, xx, kk):
        return (zz * 2 + xx) * 2 + kk

    last = depth - 1
    inner = jnp.minimum(z, last - z)
    side = 1 - 2 * (2 * z // depth)

    def plane(step):
        turns = z + (1 - 2 * (step % 2)) * ((step + 1) // 2)
        return jnp.where(step <= 2 * inner, turns, z + side * (step - inner))

    def resp_copy(block):
        rows = pl.ds(block * held, held)
        return pltpu.make_async_copy(
            resp_ref.at[:, rows, :], resp.at[:, rows, :], resp_sem.at[block]
        )

    def send(block, sem, target):
        return pltpu.make_async_remote_copy(
            src_ref=spec.at[block],
            dst_ref=spec.at[block],
            send_sem=sem,
            recv_sem=block_sem.at[block],
            device_id={"dm": target},
            device_id_type=MESH,
        )

    def up(origin):
        return send(place(origin, x, k), up_sem.at[origin], place(z + 1, x, k))

    def down(origin):
        return send(place(origin, x, k), down_sem.at[origin], place(z - 1, x, k))

    def near(step):
        return send(place(plane(step), x, k), near_sem.at[step], place(z, 1 - x, k))

    def across(step, side):
        column = (x + side) % 2
        block = place(plane(step), column, k)
        return send(block, core_sem.at[step * 2 + side], place(z, x, 1 - k))

    def arrived(block):
        pltpu.make_async_copy(spec.at[block], spec.at[block], block_sem.at[block]).wait()

    def beam_copy(offset, start, count):
        other = (beam + offset) % beams
        first = beam * (dm * span) + start
        return pltpu.make_async_remote_copy(
            src_ref=stage.at[other, pl.ds(start, count), :],
            dst_ref=out_ref.at[pl.ds(first, count), :],
            send_sem=beam_send.at[offset - 1],
            recv_sem=beam_recv.at[offset - 1],
            device_id={"beam": other},
            device_id_type=MESH,
        )

    def fetch(step, carry):
        plane_at = plane(step // 4)
        resp_copy(place(plane_at, (x + step % 4 // 2) % 2, (k + step % 2) % 2)).start()
        return carry

    inputs = [
        pltpu.make_async_copy(source, target, in_sem.at[i])
        for i, (source, target) in enumerate(
            [(volt_hbm, volt_ref), (fwd_hbm, fwd_ref), (bwd_hbm, bwd_ref), (chirp_hbm, chirp_ref)]
        )
    ]
    for copy in inputs:
        copy.start()
    lax.fori_loop(0, dm, fetch, 0)

    barrier = pltpu.get_barrier_semaphore()

    @pl.when(z < last)
    def _():
        pl.semaphore_signal(
            barrier, inc=1, device_id={"dm": place(z + 1, x, k)}, device_id_type=MESH
        )

    @pl.when(z > 0)
    def _():
        pl.semaphore_signal(
            barrier, inc=1, device_id={"dm": place(z - 1, x, k)}, device_id_type=MESH
        )

    pl.semaphore_signal(barrier, inc=1, device_id={"dm": place(z, 1 - x, k)}, device_id_type=MESH)
    pl.semaphore_signal(barrier, inc=1, device_id={"dm": place(z, x, 1 - k)}, device_id_type=MESH)
    for offset in range(1, beams):
        pl.semaphore_signal(
            barrier, inc=1, device_id={"beam": (beam + offset) % beams}, device_id_type=MESH
        )

    inputs[0].wait()
    inputs[1].wait()
    rows_in[...] = volt_ref[...].astype(jnp.float32)
    stride = 2 * beams * tiles * 2
    pieces = []
    for b in range(beams):
        for parity in range(2):
            first = (parity * beams + b) * tiles * 2
            pieces.append(jnp.concatenate(
                [rows_in[pl.ds(first + t * 2 + part, half, stride=stride), :]
                 for part in range(2) for t in range(tiles)], 1))
    signal = jnp.concatenate(pieces, 0).astype(jnp.bfloat16)
    spec[me] = jnp.dot(
        signal, fwd_ref[...], preferred_element_type=jnp.float32
    ).astype(jnp.bfloat16)

    pl.semaphore_wait(barrier, 1 + beams + jnp.minimum(z, 1) + jnp.minimum(last - z, 1))

    @pl.when(z < last)
    def _():
        up(z).start()

    @pl.when(z > 0)
    def _():
        down(z).start()

    near(0).start()
    across(0, 0).start()
    inputs[2].wait()
    inputs[3].wait()

    column = lax.broadcasted_iota(jnp.int32, (1, length), 1)
    bins = length // RATE
    sample = column % bins * RATE + column // bins
    low = lax.broadcasted_iota(jnp.int32, (half, LANES), 1) < bins

    def detect(block):
        for d in range(trials):
            filt[d] = resp[d, pl.ds(block * held, held), :].astype(jnp.float32)
        for d in range(trials):
            taps = [[jnp.concatenate(
                [filt[d, pl.ds((parity * tiles + t) * 2 + part, half, stride=4 * tiles), :]
                 for t in range(tiles)], 1) for part in range(2)] for parity in range(2)]
            values = spec[block].astype(jnp.float32)
            pieces = []
            for b in range(beams):
                for parity in range(2):
                    at = (b * 2 + parity) * half
                    xr = values[at:at + half, :length]
                    xi = values[at:at + half, length:]
                    hr, hi = taps[parity]
                    pieces.append(
                        jnp.concatenate([hr * xr - hi * xi, hr * xi + hi * xr], 1)
                    )
            joined = jnp.concatenate(pieces, 0).astype(jnp.bfloat16)
            series = jnp.dot(joined, bwd_ref[...], preferred_element_type=jnp.float32)
            power = series[:, :length] * series[:, :length] + series[:, length:] * series[:, length:]
            power = jnp.where(sample >= chirp_ref[d], power, 0.0)
            total = power[:, :LANES]
            for t in range(1, tiles):
                total = total + power[:, t * LANES:(t + 1) * LANES]
            for b in range(beams):
                at = b * 2 * half
                even = total[at:at + half]
                odd = total[at + half:at + 2 * half]
                straight = jnp.where(low, even, odd)
                turned = pltpu.roll(jnp.where(low, odd, even), bins, 1)
                rows_out[b, pl.ds(d, half, stride=trials), :] = (straight + turned) * (1.0 / RATE)
        for b in range(beams):
            stage[b, pl.ds(block * span, span), :] = rows_out[b].astype(jnp.bfloat16)

    def body(step, carry):
        group, turn = step // 4, step % 4
        block = place(plane(group), (x + turn // 2) % 2, (k + turn % 2) % 2)

        @pl.when((turn == 2) & (group < last) & (z > group))
        def _():
            arrived(place(z - group - 1, x, k))

        @pl.when((turn == 2) & (group < last) & (z > group) & (z < last))
        def _():
            up(z - group - 1).start()

        @pl.when((turn == 2) & (group < last) & (z + group < last))
        def _():
            arrived(place(z + group + 1, x, k))

        @pl.when((turn == 2) & (group < last) & (z + group < last) & (z > 0))
        def _():
            down(z + group + 1).start()

        @pl.when((turn == 2) & (group < last))
        def _():
            near(group + 1).start()
            across(group + 1, 0).start()

        @pl.when(turn > 0)
        def _():
            arrived(block)

        @pl.when(turn == 2)
        def _():
            across(group, 1).start()

        resp_copy(block).wait()
        detect(block)
        for offset in range(1, beams):
            beam_copy(offset, block * span, span).start()
        return carry

    lax.fori_loop(0, dm, body, 0)

    own = pltpu.make_async_copy(
        stage.at[beam], out_ref.at[pl.ds(beam * (dm * span), dm * span), :], own_sem
    )
    own.start()

    for step in range(depth):
        @pl.when((z < last) & (z >= step))
        def _(step=step):
            up(step).wait_send()

        @pl.when((z > 0) & (z <= step))
        def _(step=step):
            down(step).wait_send()

    for step in range(depth):
        near(step).wait_send()
        across(step, 0).wait_send()
        across(step, 1).wait_send()
    own.wait()
    for offset in range(1, beams):
        whole = beam_copy(offset, 0, dm * span)
        whole.wait_send()
        whole.wait_recv()


def shards(dm, beams, voltages, responses, chirp_len):
    chans, _, _, length = voltages.shape
    trials, group = responses.shape[:2]
    tiles = length // LANES
    forward, backward = dft_tables(length)

    def tiled(array):
        head = array.shape[:-2]
        array = array.reshape(head + (2, tiles, LANES))
        return jnp.swapaxes(array, -2, -3)

    volt = tiled(voltages).reshape(chans * beams * tiles * 2, LANES)
    resp = tiled(responses).reshape(trials, group * tiles * 2, LANES)
    span = chans // 2 * trials
    rows = beams * dm * span
    anywhere = pl.BlockSpec(memory_space=pl.ANY)
    flops = 2 * (trials * group + chans) * beams * (2 * length) ** 2
    out = pl.pallas_call(
        functools.partial(kernel, dm, beams, trials, chans, length),
        out_shape=jax.ShapeDtypeStruct((rows, LANES), jnp.bfloat16),
        in_specs=[pl.BlockSpec(memory_space=pltpu.HBM)] * 5,
        out_specs=anywhere,
        scratch_shapes=[
            pltpu.VMEM(volt.shape, jnp.bfloat16),
            pltpu.SMEM(chirp_len.shape, jnp.int32),
            pltpu.VMEM(forward.shape, jnp.bfloat16),
            pltpu.VMEM(backward.shape, jnp.bfloat16),
            pltpu.VMEM((dm, beams * chans, 2 * length), jnp.bfloat16),
            pltpu.VMEM(resp.shape, jnp.bfloat16),
            pltpu.VMEM((beams, dm * span, LANES), jnp.bfloat16),
            pltpu.VMEM(volt.shape, jnp.float32),
            pltpu.VMEM((trials, chans * tiles * 2, LANES), jnp.float32),
            pltpu.VMEM((beams, span, LANES), jnp.float32),
            pltpu.SemaphoreType.DMA((dm,)),
            pltpu.SemaphoreType.DMA((dm // 4,)),
            pltpu.SemaphoreType.DMA((dm // 4,)),
            pltpu.SemaphoreType.DMA((dm // 4,)),
            pltpu.SemaphoreType.DMA((dm // 2,)),
            pltpu.SemaphoreType.DMA((dm,)),
            pltpu.SemaphoreType.DMA((beams,)),
            pltpu.SemaphoreType.DMA((beams,)),
            pltpu.SemaphoreType.DMA,
            pltpu.SemaphoreType.DMA((4,)),
        ],
        compiler_params=pltpu.CompilerParams(
            collective_id=0, has_side_effects=True, vmem_limit_bytes=48 * 2**20
        ),
        cost_estimate=pl.CostEstimate(
            flops=flops, bytes_accessed=resp.size * 2 + rows * LANES * 2, transcendentals=0
        ),
    )(volt, resp, chirp_len, jnp.asarray(forward), jnp.asarray(backward))
    out = out.reshape(-1, trials, LANES)
    return jnp.swapaxes(out, 0, 1).reshape(trials, 1, -1)


def solution(mesh):
    placed = (P(("beam", "dm"), None, None, None), P("dm", "beam", None, None), P("dm"))
    return jax.shard_map(
        functools.partial(shards, mesh.shape["dm"], mesh.shape["beam"]),
        mesh=mesh, in_specs=placed, out_specs=P("dm", "beam", None), check_vma=False,
    )
```

```python
import functools
import math

import jax
import jax.numpy as jnp
import ml_dtypes
import numpy as np
from jax import lax
from jax.experimental import pallas as pl
from jax.experimental.pallas import tpu as pltpu
from jax.sharding import PartitionSpec as P

RATE = 4
LANES = 128
MESH = pl.DeviceIdType.MESH


def dft_tables(length):
    sample = np.arange(length)
    angles = (sample[:, None] * sample[None, :] % length) * (2.0 * math.pi / length)
    cosine = np.cos(angles) / math.sqrt(length)
    sine = np.sin(angles) / math.sqrt(length)
    forward = np.block([[cosine, -sine], [sine, cosine]])
    order = sample.reshape(-1, RATE).T.reshape(-1)
    cosine, sine = cosine[:, order], sine[:, order]
    backward = np.block([[cosine, sine], [-sine, cosine]])
    return [table.astype(np.float32).astype(ml_dtypes.bfloat16) for table in (forward, backward)]


def kernel(
    dm, beams, trials, chans, length,
    volt_hbm, resp_ref, chirp_hbm, fwd_hbm, bwd_hbm, out_ref,
    volt_ref, chirp_ref, fwd_ref, bwd_ref, spec, resp, stage, rows_in, filt, rows_out,
    block_sem, up_sem, down_sem, near_sem, core_sem, resp_sem, beam_send, beam_recv, own_sem, in_sem,
):
    tiles = length // LANES
    half = chans // 2
    depth = dm // 4
    span = half * trials
    held = chans * tiles * 2
    me = lax.axis_index("dm")
    beam = lax.axis_index("beam")
    z, x, k = me // 4, (me // 2) % 2, me % 2

    def place(zz, xx, kk):
        return (zz * 2 + xx) * 2 + kk

    last = depth - 1
    inner = jnp.minimum(z, last - z)
    side = 1 - 2 * (2 * z // depth)

    def plane(step):
        turns = z + (1 - 2 * (step % 2)) * ((step + 1) // 2)
        return jnp.where(step <= 2 * inner, turns, z + side * (step - inner))

    def resp_copy(block):
        rows = pl.ds(block * held, held)
        return pltpu.make_async_copy(
            resp_ref.at[:, rows, :], resp.at[:, rows, :], resp_sem.at[block]
        )

    def send(block, sem, target):
        return pltpu.make_async_remote_copy(
            src_ref=spec.at[block],
            dst_ref=spec.at[block],
            send_sem=sem,
            recv_sem=block_sem.at[block],
            device_id={"dm": target},
            device_id_type=MESH,
        )

    def up(origin):
        return send(place(origin, x, k), up_sem.at[origin], place(z + 1, x, k))

    def down(origin):
        return send(place(origin, x, k), down_sem.at[origin], place(z - 1, x, k))

    def near(step):
        return send(place(plane(step), x, k), near_sem.at[step], place(z, 1 - x, k))

    def across(step, side):
        column = (x + side) % 2
        block = place(plane(step), column, k)
        return send(block, core_sem.at[step * 2 + side], place(z, x, 1 - k))

    def arrived(block):
        pltpu.make_async_copy(spec.at[block], spec.at[block], block_sem.at[block]).wait()

    def beam_copy(offset, start, count):
        other = (beam + offset) % beams
        first = beam * (dm * span) + start
        return pltpu.make_async_remote_copy(
            src_ref=stage.at[other, pl.ds(start, count), :],
            dst_ref=out_ref.at[pl.ds(first, count), :],
            send_sem=beam_send.at[offset - 1],
            recv_sem=beam_recv.at[offset - 1],
            device_id={"beam": other},
            device_id_type=MESH,
        )

    def fetch(step, carry):
        plane_at = plane(step // 4)
        resp_copy(place(plane_at, (x + step % 4 // 2) % 2, (k + step % 2) % 2)).start()
        return carry

    inputs = [
        pltpu.make_async_copy(source, target, in_sem.at[i])
        for i, (source, target) in enumerate(
            [(volt_hbm, volt_ref), (fwd_hbm, fwd_ref), (bwd_hbm, bwd_ref), (chirp_hbm, chirp_ref)]
        )
    ]
    for copy in inputs:
        copy.start()
    lax.fori_loop(0, dm, fetch, 0)

    barrier = pltpu.get_barrier_semaphore()

    @pl.when(z < last)
    def _():
        pl.semaphore_signal(
            barrier, inc=1, device_id={"dm": place(z + 1, x, k)}, device_id_type=MESH
        )

    @pl.when(z > 0)
    def _():
        pl.semaphore_signal(
            barrier, inc=1, device_id={"dm": place(z - 1, x, k)}, device_id_type=MESH
        )

    pl.semaphore_signal(barrier, inc=1, device_id={"dm": place(z, 1 - x, k)}, device_id_type=MESH)
    pl.semaphore_signal(barrier, inc=1, device_id={"dm": place(z, x, 1 - k)}, device_id_type=MESH)
    for offset in range(1, beams):
        pl.semaphore_signal(
            barrier, inc=1, device_id={"beam": (beam + offset) % beams}, device_id_type=MESH
        )

    inputs[0].wait()
    inputs[1].wait()
    rows_in[...] = volt_ref[...].astype(jnp.float32)
    stride = 2 * beams * tiles * 2
    pieces = []
    for b in range(beams):
        for parity in range(2):
            first = (parity * beams + b) * tiles * 2
            pieces.append(jnp.concatenate(
                [rows_in[pl.ds(first + t * 2 + part, half, stride=stride), :]
                 for part in range(2) for t in range(tiles)], 1))
    signal = jnp.concatenate(pieces, 0).astype(jnp.bfloat16)
    spec[me] = jnp.dot(
        signal, fwd_ref[...], preferred_element_type=jnp.float32
    ).astype(jnp.bfloat16)

    pl.semaphore_wait(barrier, 1 + beams + jnp.minimum(z, 1) + jnp.minimum(last - z, 1))

    @pl.when(z < last)
    def _():
        up(z).start()

    @pl.when(z > 0)
    def _():
        down(z).start()

    near(0).start()
    across(0, 0).start()
    inputs[2].wait()
    inputs[3].wait()

    column = lax.broadcasted_iota(jnp.int32, (1, length), 1)
    bins = length // RATE
    sample = column % bins * RATE + column // bins
    low = lax.broadcasted_iota(jnp.int32, (half, LANES), 1) < bins

    def detect(block):
        for d in range(trials):
            filt[d] = resp[d, pl.ds(block * held, held), :].astype(jnp.float32)
        for d in range(trials):
            taps = [[jnp.concatenate(
                [filt[d, pl.ds((parity * tiles + t) * 2 + part, half, stride=4 * tiles), :]
                 for t in range(tiles)], 1) for part in range(2)] for parity in range(2)]
            values = spec[block].astype(jnp.float32)
            pieces = []
            for b in range(beams):
                for parity in range(2):
                    at = (b * 2 + parity) * half
                    xr = values[at:at + half, :length]
                    xi = values[at:at + half, length:]
                    hr, hi = taps[parity]
                    pieces.append(
                        jnp.concatenate([hr * xr - hi * xi, hr * xi + hi * xr], 1)
                    )
            joined = jnp.concatenate(pieces, 0).astype(jnp.bfloat16)
            series = jnp.dot(joined, bwd_ref[...], preferred_element_type=jnp.float32)
            power = series[:, :length] * series[:, :length] + series[:, length:] * series[:, length:]
            power = jnp.where(sample >= chirp_ref[d], power, 0.0)
            total = power[:, :LANES]
            for t in range(1, tiles):
                total = total + power[:, t * LANES:(t + 1) * LANES]
            for b in range(beams):
                at = b * 2 * half
                even = total[at:at + half]
                odd = total[at + half:at + 2 * half]
                straight = jnp.where(low, even, odd)
                turned = pltpu.roll(jnp.where(low, odd, even), bins, 1)
                rows_out[b, pl.ds(d, half, stride=trials), :] = (straight + turned) * (1.0 / RATE)
        for b in range(beams):
            stage[b, pl.ds(block * span, span), :] = rows_out[b].astype(jnp.bfloat16)

    def body(step, carry):
        group, turn = step // 4, step % 4
        block = place(plane(group), (x + turn // 2) % 2, (k + turn % 2) % 2)

        @pl.when((turn == 2) & (group < last) & (z > group))
        def _():
            arrived(place(z - group - 1, x, k))

        @pl.when((turn == 2) & (group < last) & (z > group) & (z < last))
        def _():
            up(z - group - 1).start()

        @pl.when((turn == 2) & (group < last) & (z + group < last))
        def _():
            arrived(place(z + group + 1, x, k))

        @pl.when((turn == 2) & (group < last) & (z + group < last) & (z > 0))
        def _():
            down(z + group + 1).start()

        @pl.when((turn == 2) & (group < last))
        def _():
            near(group + 1).start()
            across(group + 1, 0).start()

        @pl.when(turn > 0)
        def _():
            arrived(block)

        @pl.when(turn == 2)
        def _():
            across(group, 1).start()

        resp_copy(block).wait()
        detect(block)
        for offset in range(1, beams):
            beam_copy(offset, block * span, span).start()
        return carry

    lax.fori_loop(0, dm, body, 0)

    own = pltpu.make_async_copy(
        stage.at[beam], out_ref.at[pl.ds(beam * (dm * span), dm * span), :], own_sem
    )
    own.start()

    for step in range(depth):
        @pl.when((z < last) & (z >= step))
        def _(step=step):
            up(step).wait_send()

        @pl.when((z > 0) & (z <= step))
        def _(step=step):
            down(step).wait_send()

    for step in range(depth):
        near(step).wait_send()
        across(step, 0).wait_send()
        across(step, 1).wait_send()
    own.wait()
    for offset in range(1, beams):
        whole = beam_copy(offset, 0, dm * span)
        whole.wait_send()
        whole.wait_recv()


def shards(dm, beams, voltages, responses, chirp_len):
    chans, _, _, length = voltages.shape
    trials, group = responses.shape[:2]
    tiles = length // LANES
    forward, backward = dft_tables(length)

    def tiled(array):
        head = array.shape[:-2]
        array = array.reshape(head + (2, tiles, LANES))
        return jnp.swapaxes(array, -2, -3)

    volt = tiled(voltages).reshape(chans * beams * tiles * 2, LANES)
    resp = tiled(responses).reshape(trials, group * tiles * 2, LANES)
    span = chans // 2 * trials
    rows = beams * dm * span
    anywhere = pl.BlockSpec(memory_space=pl.ANY)
    flops = 2 * (trials * group + chans) * beams * (2 * length) ** 2
    out = pl.pallas_call(
        functools.partial(kernel, dm, beams, trials, chans, length),
        out_shape=jax.ShapeDtypeStruct((rows, LANES), jnp.bfloat16),
        in_specs=[pl.BlockSpec(memory_space=pltpu.HBM)] * 5,
        out_specs=anywhere,
        scratch_shapes=[
            pltpu.VMEM(volt.shape, jnp.bfloat16),
            pltpu.SMEM(chirp_len.shape, jnp.int32),
            pltpu.VMEM(forward.shape, jnp.bfloat16),
            pltpu.VMEM(backward.shape, jnp.bfloat16),
            pltpu.VMEM((dm, beams * chans, 2 * length), jnp.bfloat16),
            pltpu.VMEM(resp.shape, jnp.bfloat16),
            pltpu.VMEM((beams, dm * span, LANES), jnp.bfloat16),
            pltpu.VMEM(volt.shape, jnp.float32),
            pltpu.VMEM((trials, chans * tiles * 2, LANES), jnp.float32),
            pltpu.VMEM((beams, span, LANES), jnp.float32),
            pltpu.SemaphoreType.DMA((dm,)),
            pltpu.SemaphoreType.DMA((dm // 4,)),
            pltpu.SemaphoreType.DMA((dm // 4,)),
            pltpu.SemaphoreType.DMA((dm // 4,)),
            pltpu.SemaphoreType.DMA((dm // 2,)),
            pltpu.SemaphoreType.DMA((dm,)),
            pltpu.SemaphoreType.DMA((beams,)),
            pltpu.SemaphoreType.DMA((beams,)),
            pltpu.SemaphoreType.DMA,
            pltpu.SemaphoreType.DMA((4,)),
        ],
        compiler_params=pltpu.CompilerParams(
            collective_id=0, has_side_effects=True, vmem_limit_bytes=60 * 2**20
        ),
        cost_estimate=pl.CostEstimate(
            flops=flops, bytes_accessed=resp.size * 2 + rows * LANES * 2, transcendentals=0
        ),
    )(volt, resp, chirp_len, jnp.asarray(forward), jnp.asarray(backward))
    out = out.reshape(-1, trials, LANES)
    return jnp.swapaxes(out, 0, 1).reshape(trials, 1, -1)


def solution(mesh):
    placed = (P(("beam", "dm"), None, None, None), P("dm", "beam", None, None), P("dm"))
    return jax.shard_map(
        functools.partial(shards, mesh.shape["dm"], mesh.shape["beam"]),
        mesh=mesh, in_specs=placed, out_specs=P("dm", "beam", None), check_vma=False,
    )
```
